32 devices in a mesh: grp: 2 (over y), lon: 4 (over z), lat: 2 (over x), ch: 2 (over core).
Axes of the slice: x: 2, y: 2, z: 4, core: 2. Of those that a mesh axis runs over, the one named last changes fastest.
Arguments:
- fields: bfloat16 [69, 512, 512], P(None, ('grp', 'lat'), 'lon'), parts along dimension 1, may hold values from -6 to 6
- land_sea: int32 [256, 512], P('lat', 'lon'), may hold values 0 or 1
- orography: int32 [256, 512], P('lat', 'lon'), may hold values from 0 to 63
- embed_weight: bfloat16 [69, 4, 4, 512], P(None, None, None, 'ch'), may hold values from -0.1875 to 0.1875
- class_table: bfloat16 [128, 512], P(None, 'ch'), may hold values from -5 to 5
- conv_kernel: float32 [2, 7, 7, 512], P(None, None, None, 'ch'), may hold values from -1.75 to 1.75
- conv_bias: float32 [2, 512], P(None, 'ch'), may hold values from -3 to 3
- norm_gain: float32 [2, 512], replicated, may hold values from 0.5 to 1.5
- norm_bias: float32 [2, 512], replicated, may hold values from -3 to 3
- up_proj: bfloat16 [2, 512, 2048], P(None, 'lon', 'ch'), may hold values from -0.25 to 0.25
- up_bias: float32 [2, 2048], replicated, may hold values from -3 to 3
- down_proj: bfloat16 [2, 2048, 512], P(None, 'ch', 'lon'), may hold values from -0.125 to 0.125
- down_bias: float32 [2, 512], replicated, may hold values from -3 to 3
- layer_scale: float32 [2, 512], replicated, may hold values from 0.25 to 1.75
Outputs:
- features: bfloat16 [128, 128, 512], P(('grp', 'lat'), 'lon', 'ch'), parts along dimension 0
The draws below stay inside these ranges and needn't reach their ends.
There are 2 independent parts, one for each index of `grp`. The reference program is written for one: setup_inputs(seed, part) draws one part's arguments, and reference() takes and returns one part's arrays. A program takes and returns all parts, laid end to end along the dimension named above; an argument that names none is the same for every part. Nothing has to cross between parts.
All inputs are finite; a program needn't handle non-finite values. No bound on the sum of `land_sea` on one device may be relied on, other than what follows from the above.
Results may differ from the reference program's by a relative error of at most 0.014.
Values may be sent and summed in bfloat16 or wider, within the bound.
A program may use at most 64 MiB of HBM per device.

```python
import jax
import jax.numpy as jnp
from jax import lax

VARS = 69
PATCH = 4
C = 512
HID = 2048
OROG = 64
KERNEL = 7
BLOCKS = 2
HALO = 3
CLASSES = 128
NLAT = 64
NLON = 128
LATC = 256
LONC = 512


def draw_conv_kernel(key, part):
    base = jnp.clip(jax.random.normal(key, (BLOCKS, KERNEL, KERNEL, C), jnp.float32), -4.0, 4.0)
    ramp = 3.0 ** (2.0 * jnp.arange(C, dtype=jnp.float32) / C - 1.0)
    return base * ramp / KERNEL


def set_ends(entries, stream_key, least, high):
    dims = entries.shape
    index_at = [jax.random.randint(jax.random.fold_in(stream_key, axis), (), 0, dims[axis]) for axis in range(len(dims))]
    entries = entries.at[tuple(index_at)].set(least)
    longest = dims.index(max(dims))
    index_at[longest] = (index_at[longest] + 1) % dims[longest]
    return entries.at[tuple(index_at)].set(high)


def block_levels(key, extent, split, least, high):
    loudness = 1.0
    for dim, shards_of in split:
        draws = jax.random.uniform(jax.random.fold_in(jax.random.fold_in(key, 6), dim), (shards_of,), jnp.float32, least / len(split), high / len(split))
        loudness = loudness * jnp.repeat(jnp.exp(draws), extent[dim] // shards_of).reshape((-1,) + (1,) * (len(extent) - 1 - dim))
    return loudness


def gaussian(stream_key, extent, spread, reach, shards=(), kind=jnp.bfloat16):
    array = spread * jax.random.normal(stream_key, extent, jnp.float32)
    if shards:
        array = array * block_levels(stream_key, extent, shards, -0.22, 0.18)
    return jnp.clip(array, -reach, reach).astype(kind)


def setup_inputs(seed: int = 0, part: int = 0) -> dict:
    splits = jax.random.split(jax.random.key(seed), 15)
    own_keys = jax.random.split(jax.random.fold_in(splits[14], part), 15)
    return {
        "fields": gaussian(own_keys[0], (VARS, LATC, LONC), 1.0, 6.0, ((1, 2), (2, 4))),
        "land_sea": set_ends((jax.random.randint(splits[1], (LATC, LONC), 0, 10) < 3).astype(jnp.int32), jax.random.fold_in(splits[1], 1), 0, 1),
        "orography": set_ends(jax.random.randint(splits[2], (LATC, LONC), 0, OROG), jax.random.fold_in(splits[2], 1), 0, OROG - 1).astype(jnp.int32),
        "embed_weight": gaussian(splits[3], (VARS, PATCH, PATCH, C), (VARS * PATCH * PATCH) ** -0.5, 0.1875, ((3, 2),)),
        "class_table": gaussian(splits[4], (CLASSES, C), 1.0, 5.0, ((1, 2),)),
        "conv_kernel": draw_conv_kernel(jax.random.fold_in(splits[14], 71), part),
        "conv_bias": gaussian(splits[6], (BLOCKS, C), 0.5, 3.0, ((1, 2),), jnp.float32),
        "norm_gain": jnp.clip(1.0 + 0.1 * jax.random.normal(splits[7], (BLOCKS, C), jnp.float32), 0.5, 1.5),
        "norm_bias": gaussian(splits[8], (BLOCKS, C), 0.5, 3.0, (), jnp.float32),
        "up_proj": gaussian(splits[9], (BLOCKS, C, HID), C ** -0.5, 0.25, ((1, 4), (2, 2))),
        "up_bias": gaussian(splits[10], (BLOCKS, HID), 0.5, 3.0, (), jnp.float32),
        "down_proj": gaussian(splits[11], (BLOCKS, HID, C), HID ** -0.5, 0.125, ((1, 2), (2, 4))),
        "down_bias": gaussian(splits[12], (BLOCKS, C), 0.5, 3.0, (), jnp.float32),
        "layer_scale": jnp.clip(1.0 + 0.15 * jax.random.normal(splits[13], (BLOCKS, C), jnp.float32), 0.25, 1.75),
    }


def normalize(values, gain, shift):
    average = lax.optimization_barrier(jnp.sum(values, axis=-1, keepdims=True)) / C
    variance = lax.optimization_barrier(jnp.sum(values * values, axis=-1, keepdims=True)) / C - average * average
    return (values - average) * lax.rsqrt(variance + 1e-06) * gain + shift

def reference(fields, land_sea, orography, embed_weight, class_table, conv_kernel, conv_bias, norm_gain, norm_bias, up_proj, up_bias, down_proj, down_bias, layer_scale):
    class_codes = 2 * orography + land_sea
    class_rows = class_table.astype(jnp.float32)
    weight = embed_weight.astype(jnp.float32)
    cell_grid = fields.reshape(VARS, NLAT, PATCH, NLON, PATCH)

    def embed_band(band_row):
        band_block = lax.dynamic_index_in_dim(cell_grid, band_row, 1, keepdims=False).astype(jnp.float32)
        patch_term = jnp.einsum('vpcq,vpqk->ck', band_block, weight)
        code_rows = lax.dynamic_slice_in_dim(class_codes, band_row * PATCH, PATCH, 0)
        one_hot = (code_rows[..., None] == jnp.arange(CLASSES, dtype=jnp.int32)).astype(jnp.float32)
        class_counts = one_hot.reshape(PATCH, NLON, PATCH, CLASSES).sum(axis=(0, 2))
        static_term = jnp.dot(class_counts, class_rows, preferred_element_type=jnp.float32)
        return (patch_term + static_term * (1.0 / (PATCH * PATCH))).astype(jnp.bfloat16)
    stream = lax.map(embed_band, jnp.arange(NLAT, dtype=jnp.int32))
    for layer in range(BLOCKS):
        stream_f = stream.astype(jnp.float32)
        padded = jnp.pad(stream_f, ((HALO, HALO), (0, 0), (0, 0)))
        padded = jnp.concatenate([padded[:, NLON - HALO:], padded, padded[:, :HALO]], axis=1)
        summed = jnp.zeros((NLAT, NLON, C), jnp.float32) + conv_bias[layer]
        for row_off in range(KERNEL):
            for col_off in range(KERNEL):
                summed = summed + padded[row_off:row_off + NLAT, col_off:col_off + NLON] * conv_kernel[layer, row_off, col_off]
        conv = summed.astype(jnp.bfloat16)
        normed = normalize(conv.astype(jnp.float32), norm_gain[layer], norm_bias[layer]).astype(jnp.bfloat16)
        up_weight = up_proj[layer]
        down_weight = down_proj[layer]
        bias_up = up_bias[layer]

        def feed_forward(rows_in):
            pre = jnp.dot(rows_in, up_weight, preferred_element_type=jnp.float32) + bias_up
            hidden = jax.nn.gelu(pre, approximate=True).astype(jnp.bfloat16)
            return jnp.dot(hidden, down_weight, preferred_element_type=jnp.float32)
        update = lax.map(feed_forward, normed)
        stream = (stream_f + layer_scale[layer] * (update + down_bias[layer])).astype(jnp.bfloat16)
    return stream
```

```python
import jax
import jax.numpy as jnp
from jax import lax
from jax.sharding import PartitionSpec as P

PATCH = 4
KERNEL = 7
BLOCKS = 2
HALO = 3


def padded(cells, sides, width, closed):
    for axis, dim in sides:
        count = lax.axis_size(axis)
        ends = count if closed else count - 1
        head = lax.slice_in_dim(cells, 0, width, axis=dim)
        tail = lax.slice_in_dim(cells, cells.shape[dim] - width, cells.shape[dim], axis=dim)
        cells = jnp.concatenate(
            [
                lax.ppermute(tail, axis, [(i, (i + 1) % count) for i in range(ends)]),
                cells,
                lax.ppermute(head, axis, [((i + 1) % count, i) for i in range(ends)]),
            ],
            axis=dim,
        )
    return cells


def embed_tokens(fields, land_sea, orography, embed_weight, class_table):
    var_count, lat_cells, lon_cells = fields.shape
    tok_rows = lat_cells // PATCH
    tok_cols = lon_cells // PATCH
    width = embed_weight.shape[3]
    cell_grid = fields.reshape(var_count, tok_rows, PATCH, tok_cols, PATCH)
    patch_term = jnp.einsum(
        "vrpcq,vpqk->rck", cell_grid, embed_weight, preferred_element_type=jnp.float32
    )
    class_codes = 2 * orography + land_sea
    classes = class_table.shape[0]
    one_hot = (class_codes[..., None] == jnp.arange(classes, dtype=jnp.int32)).astype(jnp.bfloat16)
    class_counts = one_hot.reshape(tok_rows, PATCH, tok_cols, PATCH, classes).sum(axis=(1, 3))
    static_term = jnp.dot(
        class_counts.reshape(tok_rows * tok_cols, classes),
        class_table,
        preferred_element_type=jnp.float32,
    )
    return (
        patch_term + static_term.reshape(tok_rows, tok_cols, width) * (1.0 / (PATCH * PATCH))
    ).astype(jnp.bfloat16)


def depthwise(framed, kernel, bias, tok_rows, tok_cols):
    summed = jnp.zeros((tok_rows, tok_cols, kernel.shape[2]), jnp.float32) + bias
    for row_off in range(KERNEL):
        for col_off in range(KERNEL):
            summed = (
                summed
                + framed[row_off : row_off + tok_rows, col_off : col_off + tok_cols].astype(
                    jnp.float32
                )
                * kernel[row_off, col_off]
            )
    return summed.astype(jnp.bfloat16)


def gather_rows(weight, spare):
    count = lax.axis_size(spare)
    rows = weight.shape[0] // count
    share = lax.dynamic_slice_in_dim(weight, lax.axis_index(spare) * rows, rows)
    return lax.all_gather(share, ("lon", spare), axis=0, tiled=True)


def body(
    fields,
    land_sea,
    orography,
    embed_weight,
    class_table,
    conv_kernel,
    conv_bias,
    norm_gain,
    norm_bias,
    up_proj,
    up_bias,
    down_proj,
    down_bias,
    layer_scale,
):
    var_count, lat_cells, lon_cells = fields.shape
    tok_rows = lat_cells // PATCH
    tok_cols = lon_cells // PATCH
    channels = norm_gain.shape[1]
    core_index = lax.axis_index("ch")
    token_count = tok_rows * tok_cols
    half_width = embed_weight.shape[3]
    hid = up_proj.shape[2]
    sectors = lax.axis_size("lon")
    weights = []
    for layer in range(BLOCKS):
        up = gather_rows(up_proj[layer], "lat")
        down = gather_rows(down_proj[layer], "grp").reshape(sectors, hid, channels // sectors)
        weights.append((up, down))
    stream = embed_tokens(fields, land_sea, orography, embed_weight, class_table)
    for layer in range(BLOCKS):
        sector_ext = padded(stream, (("lon", 1),), HALO, True)
        framed = padded(sector_ext, (("lat", 0),), HALO, False)
        conv = depthwise(framed, conv_kernel[layer], conv_bias[layer], tok_rows, tok_cols).reshape(
            token_count, half_width
        )
        conv_f = lax.all_gather(conv, "ch", axis=1, tiled=True).astype(jnp.float32)
        average = jnp.sum(conv_f, axis=1, keepdims=True) / channels
        variance = jnp.sum(conv_f * conv_f, axis=1, keepdims=True) / channels - average * average
        normed = (
            (conv_f - average) * lax.rsqrt(variance + 1e-06) * norm_gain[layer] + norm_bias[layer]
        ).astype(jnp.bfloat16)
        up, down = weights[layer]
        bias_up = lax.dynamic_slice_in_dim(up_bias[layer], core_index * hid, hid)
        pre = jnp.dot(normed, up, preferred_element_type=jnp.float32)
        hidden = jax.nn.gelu(pre + bias_up, approximate=True).astype(jnp.bfloat16)
        partial_sum = jnp.einsum(
            "th,zhk->tzk", hidden, down, preferred_element_type=jnp.float32
        ).reshape(token_count, channels)
        mine = lax.dynamic_slice_in_dim(partial_sum, core_index * half_width, half_width, axis=1)
        other = lax.dynamic_slice_in_dim(
            partial_sum, (1 - core_index) * half_width, half_width, axis=1
        ).astype(jnp.bfloat16)
        update = mine + lax.ppermute(other, "ch", [(0, 1), (1, 0)]).astype(jnp.float32)
        bias_down = lax.dynamic_slice_in_dim(down_bias[layer], core_index * half_width, half_width)
        scale_share = lax.dynamic_slice_in_dim(
            layer_scale[layer], core_index * half_width, half_width
        )
        stream_f = stream.reshape(token_count, half_width).astype(jnp.float32)
        stream = (
            (stream_f + scale_share * (update + bias_down))
            .astype(jnp.bfloat16)
            .reshape(tok_rows, tok_cols, half_width)
        )
    return stream


def solution(mesh):
    in_specs = (
        P(None, ("grp", "lat"), "lon"),
        P("lat", "lon"),
        P("lat", "lon"),
        P(None, None, None, "ch"),
        P(None, "ch"),
        P(None, None, None, "ch"),
        P(None, "ch"),
        P(),
        P(),
        P(None, "lon", "ch"),
        P(),
        P(None, "ch", "lon"),
        P(),
        P(),
    )
    out_specs = P(("grp", "lat"), "lon", "ch")
    return jax.shard_map(body, mesh=mesh, in_specs=in_specs, out_specs=out_specs, check_vma=False)
```

```python
import functools

import jax
import jax.numpy as jnp
import numpy as np
from jax import lax
from jax.experimental import pallas as pl
from jax.experimental.pallas import tpu as pltpu
from jax.sharding import PartitionSpec as P

PATCH = 4
KERNEL = 7
BLOCKS = 2
HALO = 3


def embed_tokens(fields, land_sea, orography, embed_weight, class_table):
    var_count, lat_cells, lon_cells = fields.shape
    tok_rows = lat_cells // PATCH
    tok_cols = lon_cells // PATCH
    width = embed_weight.shape[3]
    cell_grid = fields.reshape(var_count, tok_rows, PATCH, tok_cols, PATCH)
    patch_term = jnp.einsum(
        "vrpcq,vpqk->rck", cell_grid, embed_weight, preferred_element_type=jnp.float32
    )
    class_codes = 2 * orography + land_sea
    classes = class_table.shape[0]
    one_hot = (class_codes[..., None] == jnp.arange(classes, dtype=jnp.int32)).astype(jnp.bfloat16)
    class_counts = one_hot.reshape(tok_rows, PATCH, tok_cols, PATCH, classes).sum(axis=(1, 3))
    static_term = jnp.dot(
        class_counts.reshape(tok_rows * tok_cols, classes),
        class_table,
        preferred_element_type=jnp.float32,
    )
    return (
        patch_term + static_term.reshape(tok_rows, tok_cols, width) * (1.0 / (PATCH * PATCH))
    ).astype(jnp.bfloat16)


LEFT = 8
CORNER = 16
DIRECTIONS = tuple(
    (dx, dz) for dx in (-1, 0, 1) for dz in (-1, 0, 1) if (dx, dz) != (0, 0)
)
CORNERS = tuple(d for d in DIRECTIONS if d[0] and d[1])


def edge_maps(rows, cols):
    side = HALO * rows
    total = 2 * side + CORNER * len(CORNERS)
    pack = np.zeros((total, rows * cols), np.float32)
    spread = np.zeros((2, rows + 2 * HALO, LEFT, total), np.float32)
    for way, dz in enumerate((-1, 1)):
        first = cols - HALO if dz > 0 else 0
        lane = LEFT - HALO if dz > 0 else 0
        rim = 0 if dz > 0 else 1
        for c in range(HALO):
            for r in range(rows):
                slot = way * side + c * rows + r
                pack[slot, r * cols + first + c] = 1
                spread[rim, HALO + r, lane + c, slot] = 1
            for k, (dx, kz) in enumerate(CORNERS):
                if kz != dz:
                    continue
                for i in range(HALO):
                    slot = 2 * side + CORNER * k + c * HALO + i
                    r = rows - HALO + i if dx > 0 else i
                    pack[slot, r * cols + first + c] = 1
                    spread[rim, i if dx > 0 else rows + HALO + i, lane + c, slot] = 1
    return pack, spread.reshape(-1, total)


def kernel_body(
    rows,
    cols,
    stream_in,
    pack,
    spread,
    conv_kernel,
    conv_bias,
    norm_gain,
    norm_bias,
    weight_in,
    up_bias,
    down_bias,
    layer_scale,
    out,
    stream,
    edges,
    rim,
    band,
    frame,
    shifted,
    conv_all,
    weights,
    mine,
    outgoing,
    incoming,
    halo_send,
    halo_recv,
    z_send,
    z_recv,
    h_send,
    h_recv,
    conv_send,
    conv_recv,
    part_send,
    part_recv,
):
    lats, lons, grps = lax.axis_size("lat"), lax.axis_size("lon"), lax.axis_size("grp")
    x, z, y, core = (lax.axis_index(n) for n in ("lat", "lon", "grp", "ch"))
    tokens, half = rows * cols, stream.shape[1]
    channels = norm_gain.shape[1]
    hid = weights.shape[2]
    share = weight_in.shape[1]
    side = HALO * rows
    partner = {"ch": 1 - core}
    mesh_ids = pl.DeviceIdType.MESH

    def remote(src, dst, send, recv, device):
        return pltpu.make_async_remote_copy(
            src_ref=src,
            dst_ref=dst,
            send_sem=send,
            recv_sem=recv,
            device_id=device,
            device_id_type=mesh_ids,
        )

    def helper(m):
        name, count, index = (("lat", lats, x), ("grp", grps, y))[m % 2]
        if share % (16 * count):
            return name, 1, 0
        return name, count, index

    def piece(m, owner, index):
        count = helper(m)[1]
        part = share // count
        start = pl.multiple_of(owner * share + index * part, 16)
        return weights.at[m, pl.ds(start, part)]

    def z_copy(m, dz):
        ref = piece(m, z, helper(m)[2])
        return remote(
            ref, ref, z_send.at[m, dz - 1], z_recv.at[m, dz - 1], {"lon": lax.rem(z + dz, lons)}
        )

    def z_landed(m, dz):
        ref = piece(m, lax.rem(z - dz + lons, lons), helper(m)[2])
        return remote(
            ref, ref, z_send.at[m, dz - 1], z_recv.at[m, dz - 1], {"lon": lax.rem(z + dz, lons)}
        )

    def h_copy(m, dz, dh, back):
        name, count, index = helper(m)
        owner = lax.rem(z - dz + lons, lons)
        ref = piece(m, owner, lax.rem(index - dh + count, count) if back else index)
        return remote(
            ref,
            ref,
            h_send.at[m, dz - 1, dh - 1],
            h_recv.at[m, dz - 1, dh - 1],
            {name: lax.rem(index + dh, count)},
        )

    def send_weights(layer):
        for dz in range(1, lons):
            for m in (2 * layer, 2 * layer + 1):
                z_copy(m, dz).start()

    def pass_on(layer, dz):
        for m in (2 * layer, 2 * layer + 1):
            z_landed(m, dz).wait_recv()
            for dh in range(1, helper(m)[1]):
                h_copy(m, dz, dh, False).start()

    def finish_weights(layer):
        for m in (2 * layer, 2 * layer + 1):
            for dz in range(1, lons):
                z_copy(m, dz).wait_send()
                for dh in range(1, helper(m)[1]):
                    h_copy(m, dz, dh, False).wait_send()
                    h_copy(m, dz, dh, True).wait_recv()

    def halo_copy(layer, k):
        dx, dz = DIRECTIONS[k]
        if dz == 0:
            src = stream.at[pl.ds((rows - HALO if dx > 0 else 0) * cols, HALO * cols)]
            dst = band.at[layer, 0 if dx > 0 else 1]
        else:
            if dx == 0:
                where = pl.ds(0 if dz < 0 else side, side)
            else:
                where = pl.ds(2 * side + CORNER * CORNERS.index((dx, dz)), CORNER)
            src, dst = edges.at[layer, where], rim.at[layer, where]
        device = {"lat": x + dx, "lon": lax.rem(z + dz + lons, lons)}
        return remote(src, dst, halo_send.at[layer, k], halo_recv.at[layer, k], device)

    def each_halo(layer, act, arriving):
        for k, (dx, _) in enumerate(DIRECTIONS):
            where = x - dx if arriving else x + dx
            if dx == 0:
                act(halo_copy(layer, k))
            else:

                @pl.when((where >= 0) & (where < lats))
                def _():
                    act(halo_copy(layer, k))

    barrier = pltpu.get_barrier_semaphore()

    def greet(device):
        pl.semaphore_signal(barrier, inc=1, device_id=device, device_id_type=mesh_ids)

    rim[...] = jnp.zeros_like(rim)
    band[...] = jnp.zeros_like(band)
    for k, (dx, dz) in enumerate(DIRECTIONS):
        device = {"lat": x + dx, "lon": lax.rem(z + dz + lons, lons)}
        if dx == 0:
            greet(device)
        else:

            @pl.when((x + dx >= 0) & (x + dx < lats))
            def _():
                greet(device)

    for dz in range(1, lons):
        greet({"lon": lax.rem(z + dz, lons)})
    for dx in range(1, lats):
        greet({"lat": lax.rem(x + dx, lats)})
    for dy in range(1, grps):
        greet({"grp": lax.rem(y + dy, grps)})
    greet(partner)
    owed = 2 + (lons - 1) + (lats - 1) + (grps - 1) + 1
    inner = (x > 0).astype(jnp.int32) + (x < lats - 1).astype(jnp.int32)
    stream[...] = stream_in[...]
    mine_rows = pl.ds(pl.multiple_of(z * share, 16), share)
    for m in range(2 * BLOCKS):
        weights[m, mine_rows] = weight_in[m]

    for layer in range(BLOCKS):
        edges[layer] = jnp.dot(
            pack[...], stream[...], preferred_element_type=jnp.float32
        ).astype(jnp.bfloat16)
        if layer == 0:
            pl.semaphore_wait(barrier, owed + 3 * inner)
        each_halo(layer, lambda c: c.start(), False)
        if layer == 0:
            send_weights(0)
        frame[HALO : HALO + rows, LEFT : LEFT + cols] = (
            stream[...].astype(jnp.float32).reshape(rows, cols, half)
        )
        each_halo(layer, lambda c: c.wait_recv(), True)
        ends = jnp.dot(spread[...], rim[layer], preferred_element_type=jnp.float32).reshape(
            2, rows + 2 * HALO, LEFT, half
        )
        frame[:, :LEFT] = ends[0]
        frame[:, LEFT + cols :] = ends[1]
        for end, first in ((0, 0), (1, HALO + rows)):
            frame[first : first + HALO, LEFT : LEFT + cols] = (
                band[layer, end].astype(jnp.float32).reshape(HALO, cols, half)
            )

        def shift_row(r, _):
            line = frame[r]
            for e in range(KERNEL):
                first = LEFT - HALO + e
                shifted[e, r] = line[first : first + cols]
            return 0

        lax.fori_loop(0, rows + 2 * HALO, shift_row, 0)

        def conv_row(i, _):
            total = jnp.broadcast_to(conv_bias[layer, 0], (cols, half))
            for a in range(KERNEL):
                for e in range(KERNEL):
                    total = total + shifted[e, i + a] * conv_kernel[layer, a, e]
            at = pl.ds(pl.multiple_of(i * cols, 16), cols)
            conv_all[layer, core, at] = total.astype(jnp.bfloat16)
            return 0

        quarters = 4
        step = rows // quarters
        order = [1, lons - 1] + list(range(2, lons - 1))
        order = order[: lons - 1]

        def conv_copy(q):
            at = pl.ds(q * step * cols, step * cols)
            ref = conv_all.at[layer, core, at]
            return remote(ref, ref, conv_send.at[layer, q], conv_recv.at[layer, q], partner)

        def conv_landed(q):
            at = pl.ds(q * step * cols, step * cols)
            ref = conv_all.at[layer, 1 - core, at]
            return remote(ref, ref, conv_send.at[layer, q], conv_recv.at[layer, q], partner)

        for q in range(quarters):
            lax.fori_loop(q * step, (q + 1) * step, conv_row, 0)
            conv_copy(q).start()
            if q:
                cut = len(order)
                for dz in order[(q - 1) * cut // 3 : q * cut // 3]:
                    pass_on(layer, dz)
        if layer + 1 < BLOCKS:
            send_weights(layer + 1)
        finish_weights(layer)
        for q in range(quarters):
            conv_landed(q).wait_recv()
            conv_copy(q).wait_send()
        each_halo(layer, lambda c: c.wait_send(), False)

        chunk = step * cols

        def part_copy(c):
            at = pl.ds(pl.multiple_of(c * chunk, 16), chunk)
            return remote(
                outgoing.at[layer, at],
                incoming.at[layer, at],
                part_send.at[layer, c],
                part_recv.at[layer, c],
                partner,
            )

        up, down = 2 * layer, 2 * layer + 1
        own = pl.ds(pl.multiple_of(core * half, 128), half)
        other = pl.ds(pl.multiple_of((1 - core) * half, 128), half)
        contract = (((1,), (1,)), ((), ()))

        def ffn(c, _):
            at = pl.ds(pl.multiple_of(c * chunk, 16), chunk)
            conv_f = jnp.concatenate(
                [conv_all[layer, 0, at], conv_all[layer, 1, at]], axis=1
            ).astype(jnp.float32)
            average = jnp.sum(conv_f, axis=1, keepdims=True) / channels
            variance = (
                jnp.sum(conv_f * conv_f, axis=1, keepdims=True) / channels - average * average
            )
            normed = (
                (conv_f - average) * lax.rsqrt(variance + 1e-06) * norm_gain[layer : layer + 1]
                + norm_bias[layer : layer + 1]
            ).astype(jnp.bfloat16)
            pre = jnp.dot(normed, weights[up], preferred_element_type=jnp.float32)
            pre = pre + up_bias[layer : layer + 1, pl.ds(pl.multiple_of(core * hid, 128), hid)]
            hidden = jax.nn.gelu(pre, approximate=True).astype(jnp.bfloat16)
            outgoing[layer, at] = lax.dot_general(
                hidden, weights[down, other], contract, preferred_element_type=jnp.float32
            ).astype(jnp.bfloat16)
            part_copy(c).start()
            mine[at] = lax.dot_general(
                hidden, weights[down, own], contract, preferred_element_type=jnp.float32
            )
            return 0

        lax.fori_loop(0, quarters, ffn, 0)

        def merge(c, _):
            at = pl.ds(pl.multiple_of(c * chunk, 16), chunk)
            part_copy(c).wait_recv()
            update = mine[at] + incoming[layer, at].astype(jnp.float32)
            fresh = stream[at].astype(jnp.float32) + layer_scale[layer : layer + 1, own] * (
                update + down_bias[layer : layer + 1, own]
            )
            if layer + 1 < BLOCKS:
                stream[at] = fresh.astype(jnp.bfloat16)
            else:
                out[at] = fresh.astype(jnp.bfloat16)
            part_copy(c).wait_send()
            return 0

        lax.fori_loop(0, quarters, merge, 0)


def body(
    fields,
    land_sea,
    orography,
    embed_weight,
    class_table,
    conv_kernel,
    conv_bias,
    norm_gain,
    norm_bias,
    up_proj,
    up_bias,
    down_proj,
    down_bias,
    layer_scale,
):
    var_count, lat_cells, lon_cells = fields.shape
    rows = lat_cells // PATCH
    cols = lon_cells // PATCH
    tokens = rows * cols
    channels = norm_gain.shape[1]
    half = embed_weight.shape[3]
    hid = up_proj.shape[2]
    lats, lons, grps = lax.axis_size("lat"), lax.axis_size("lon"), lax.axis_size("grp")
    stream = embed_tokens(fields, land_sea, orography, embed_weight, class_table)
    pack, spread = edge_maps(rows, cols)
    packed = pack.shape[0]
    weight_in = jnp.stack(
        [w for b in range(BLOCKS) for w in (up_proj[b], down_proj[b].T)]
    )
    arrays = 2 * BLOCKS
    helpers = max(lats, grps, 2) - 1
    vmem = pl.BlockSpec(memory_space=pltpu.VMEM)
    dma = pltpu.SemaphoreType.DMA
    result = pl.pallas_call(
        functools.partial(kernel_body, rows, cols),
        out_shape=jax.ShapeDtypeStruct((tokens, half), jnp.bfloat16),
        in_specs=[vmem] * 11,
        out_specs=vmem,
        scratch_shapes=[
            pltpu.VMEM((tokens, half), jnp.bfloat16),
            pltpu.VMEM((BLOCKS, packed, half), jnp.bfloat16),
            pltpu.VMEM((BLOCKS, packed, half), jnp.bfloat16),
            pltpu.VMEM((BLOCKS, 2, HALO * cols, half), jnp.bfloat16),
            pltpu.VMEM((rows + 2 * HALO, cols + 2 * LEFT, half), jnp.float32),
            pltpu.VMEM((KERNEL, rows + 2 * HALO, cols, half), jnp.float32),
            pltpu.VMEM((BLOCKS, 2, tokens, half), jnp.bfloat16),
            pltpu.VMEM((arrays, channels, hid), jnp.bfloat16),
            pltpu.VMEM((tokens, half), jnp.float32),
            pltpu.VMEM((BLOCKS, tokens, half), jnp.bfloat16),
            pltpu.VMEM((BLOCKS, tokens, half), jnp.bfloat16),
            dma((BLOCKS, len(DIRECTIONS))),
            dma((BLOCKS, len(DIRECTIONS))),
            dma((arrays, lons - 1)),
            dma((arrays, lons - 1)),
            dma((arrays, lons - 1, helpers)),
            dma((arrays, lons - 1, helpers)),
            dma((BLOCKS, 4)),
            dma((BLOCKS, 4)),
            dma((BLOCKS, 4)),
            dma((BLOCKS, 4)),
        ],
        compiler_params=pltpu.CompilerParams(
            collective_id=0, has_side_effects=True, vmem_limit_bytes=48 * 1024 * 1024
        ),
    )(
        stream.reshape(tokens, half),
        jnp.asarray(pack, jnp.bfloat16),
        jnp.asarray(spread, jnp.bfloat16),
        conv_kernel,
        conv_bias.reshape(BLOCKS, 1, half),
        norm_gain,
        norm_bias,
        weight_in,
        up_bias,
        down_bias,
        layer_scale,
    )
    return result.reshape(rows, cols, half)


def solution(mesh):
    in_specs = (
        P(None, ("grp", "lat"), "lon"),
        P("lat", "lon"),
        P("lat", "lon"),
        P(None, None, None, "ch"),
        P(None, "ch"),
        P(None, None, None, "ch"),
        P(None, "ch"),
        P(),
        P(),
        P(None, "lon", "ch"),
        P(),
        P(None, "ch", "lon"),
        P(),
        P(),
    )
    out_specs = P(("grp", "lat"), "lon", "ch")
    return jax.shard_map(body, mesh=mesh, in_specs=in_specs, out_specs=out_specs, check_vma=False)
```

```python
import functools

import jax
import jax.numpy as jnp
import numpy as np
from jax import lax
from jax.experimental import pallas as pl
from jax.experimental.pallas import tpu as pltpu
from jax.sharding import PartitionSpec as P

PATCH = 4
KERNEL = 7
BLOCKS = 2
HALO = 3


def token_cells(fields, land_sea, orography):
    var_count, lat_cells, lon_cells = fields.shape
    rows, cols = lat_cells // PATCH, lon_cells // PATCH
    grid = fields.reshape(var_count, rows, PATCH, cols, PATCH)
    patches = grid.transpose(2, 4, 1, 3, 0).reshape(PATCH * PATCH, rows * cols, var_count)
    codes = (2 * orography + land_sea).reshape(rows, PATCH, cols, PATCH)
    codes = codes.transpose(0, 2, 1, 3).reshape(rows * cols, PATCH * PATCH)
    return patches, codes


LEFT = 8
CORNER = 16
DIRECTIONS = tuple(
    (dx, dz) for dx in (-1, 0, 1) for dz in (-1, 0, 1) if (dx, dz) != (0, 0)
)
CORNERS = tuple(d for d in DIRECTIONS if d[0] and d[1])


def edge_maps(rows, cols):
    side = HALO * rows
    total = 2 * side + CORNER * len(CORNERS)
    pack = np.zeros((total, rows * cols), np.float32)
    spread = np.zeros((2, rows + 2 * HALO, LEFT, total), np.float32)
    for way, dz in enumerate((-1, 1)):
        first = cols - HALO if dz > 0 else 0
        lane = LEFT - HALO if dz > 0 else 0
        rim = 0 if dz > 0 else 1
        for c in range(HALO):
            for r in range(rows):
                slot = way * side + c * rows + r
                pack[slot, r * cols + first + c] = 1
                spread[rim, HALO + r, lane + c, slot] = 1
            for k, (dx, kz) in enumerate(CORNERS):
                if kz != dz:
                    continue
                for i in range(HALO):
                    slot = 2 * side + CORNER * k + c * HALO + i
                    r = rows - HALO + i if dx > 0 else i
                    pack[slot, r * cols + first + c] = 1
                    spread[rim, i if dx > 0 else rows + HALO + i, lane + c, slot] = 1
    return pack, spread.reshape(-1, total)


def kernel_body(
    rows,
    cols,
    patches,
    codes,
    embed_weight,
    class_table,
    pack,
    spread,
    conv_kernel,
    conv_bias,
    norm_gain,
    norm_bias,
    up_proj,
    down_proj,
    up_bias,
    down_bias,
    layer_scale,
    out,
    stream,
    edges,
    rim,
    band,
    frame,
    shifted,
    conv_all,
    weights,
    mine,
    outgoing,
    incoming,
    halo_send,
    halo_recv,
    z_send,
    z_recv,
    h_send,
    h_recv,
    conv_send,
    conv_recv,
    part_send,
    part_recv,
):
    lats, lons, grps = lax.axis_size("lat"), lax.axis_size("lon"), lax.axis_size("grp")
    x, z, y, core = (lax.axis_index(n) for n in ("lat", "lon", "grp", "ch"))
    tokens, half = rows * cols, stream.shape[1]
    channels = norm_gain.shape[1]
    hid = weights.shape[2]
    share = up_proj.shape[1]
    side = HALO * rows
    partner = {"ch": 1 - core}
    mesh_ids = pl.DeviceIdType.MESH

    def remote(src, dst, send, recv, device):
        return pltpu.make_async_remote_copy(
            src_ref=src,
            dst_ref=dst,
            send_sem=send,
            recv_sem=recv,
            device_id=device,
            device_id_type=mesh_ids,
        )

    def helper(m):
        name, count, index = (("lat", lats, x), ("grp", grps, y))[m % 2]
        if share % (16 * count):
            return name, 1, 0
        return name, count, index

    def piece(m, owner, index):
        count = helper(m)[1]
        part = share // count
        start = pl.multiple_of(owner * share + index * part, 16)
        return weights.at[m, pl.ds(start, part)]

    def z_copy(m, dz):
        ref = piece(m, z, helper(m)[2])
        return remote(
            ref, ref, z_send.at[m, dz - 1], z_recv.at[m, dz - 1], {"lon": lax.rem(z + dz, lons)}
        )

    def z_landed(m, dz):
        ref = piece(m, lax.rem(z - dz + lons, lons), helper(m)[2])
        return remote(
            ref, ref, z_send.at[m, dz - 1], z_recv.at[m, dz - 1], {"lon": lax.rem(z + dz, lons)}
        )

    def h_copy(m, dz, dh, back):
        name, count, index = helper(m)
        owner = lax.rem(z - dz + lons, lons)
        ref = piece(m, owner, lax.rem(index - dh + count, count) if back else index)
        return remote(
            ref,
            ref,
            h_send.at[m, dz - 1, dh - 1],
            h_recv.at[m, dz - 1, dh - 1],
            {name: lax.rem(index + dh, count)},
        )

    def send_weights(layer):
        for dz in range(1, lons):
            for m in (2 * layer, 2 * layer + 1):
                z_copy(m, dz).start()

    def pass_on(layer, dz):
        for m in (2 * layer, 2 * layer + 1):
            z_landed(m, dz).wait_recv()
            for dh in range(1, helper(m)[1]):
                h_copy(m, dz, dh, False).start()

    def finish_weights(layer):
        for m in (2 * layer, 2 * layer + 1):
            for dz in range(1, lons):
                z_copy(m, dz).wait_send()
                for dh in range(1, helper(m)[1]):
                    h_copy(m, dz, dh, False).wait_send()
                    h_copy(m, dz, dh, True).wait_recv()

    def halo_copy(layer, k):
        dx, dz = DIRECTIONS[k]
        if dz == 0:
            src = stream.at[pl.ds((rows - HALO if dx > 0 else 0) * cols, HALO * cols)]
            dst = band.at[layer, 0 if dx > 0 else 1]
        else:
            if dx == 0:
                where = pl.ds(0 if dz < 0 else side, side)
            else:
                where = pl.ds(2 * side + CORNER * CORNERS.index((dx, dz)), CORNER)
            src, dst = edges.at[layer, where], rim.at[layer, where]
        device = {"lat": x + dx, "lon": lax.rem(z + dz + lons, lons)}
        return remote(src, dst, halo_send.at[layer, k], halo_recv.at[layer, k], device)

    def each_halo(layer, act, arriving):
        for k, (dx, _) in enumerate(DIRECTIONS):
            where = x - dx if arriving else x + dx
            if dx == 0:
                act(halo_copy(layer, k))
            else:

                @pl.when((where >= 0) & (where < lats))
                def _():
                    act(halo_copy(layer, k))

    barrier = pltpu.get_barrier_semaphore()

    def greet(device):
        pl.semaphore_signal(barrier, inc=1, device_id=device, device_id_type=mesh_ids)

    rim[...] = jnp.zeros_like(rim)
    band[...] = jnp.zeros_like(band)
    for k, (dx, dz) in enumerate(DIRECTIONS):
        device = {"lat": x + dx, "lon": lax.rem(z + dz + lons, lons)}
        if dx == 0:
            greet(device)
        else:

            @pl.when((x + dx >= 0) & (x + dx < lats))
            def _():
                greet(device)

    for dz in range(1, lons):
        greet({"lon": lax.rem(z + dz, lons)})
    for dx in range(1, lats):
        greet({"lat": lax.rem(x + dx, lats)})
    for dy in range(1, grps):
        greet({"grp": lax.rem(y + dy, grps)})
    greet(partner)
    owed = 2 + (lons - 1) + (lats - 1) + (grps - 1) + 1
    inner = (x > 0).astype(jnp.int32) + (x < lats - 1).astype(jnp.int32)
    mine_rows = pl.ds(pl.multiple_of(z * share, 16), share)
    for b in range(BLOCKS):
        weights[2 * b, mine_rows] = up_proj[b]
        weights[2 * b + 1, mine_rows] = down_proj[b].T
    pl.semaphore_wait(barrier, owed + 3 * inner)
    send_weights(0)

    piece_rows = tokens // 4

    def embed(c, _):
        at = pl.ds(pl.multiple_of(c * piece_rows, 16), piece_rows)
        classes = class_table.shape[0]
        ids = lax.broadcasted_iota(jnp.int32, (piece_rows, classes), 1)
        cells = codes[at]
        counts = jnp.zeros((piece_rows, classes), jnp.float32)
        for s in range(PATCH * PATCH):
            counts = counts + jnp.where(cells[:, s : s + 1] == ids, 1.0, 0.0)
        total = jnp.dot(
            counts.astype(jnp.bfloat16), class_table[...], preferred_element_type=jnp.float32
        ) * (1.0 / (PATCH * PATCH))
        for s in range(PATCH * PATCH):
            total = total + jnp.dot(
                patches[s, at], embed_weight[s], preferred_element_type=jnp.float32
            )
        stream[at] = total.astype(jnp.bfloat16)
        return 0

    lax.fori_loop(0, 4, embed, 0)

    for layer in range(BLOCKS):
        edges[layer] = jnp.dot(
            pack[...], stream[...], preferred_element_type=jnp.float32
        ).astype(jnp.bfloat16)
        each_halo(layer, lambda c: c.start(), False)
        frame[HALO : HALO + rows, LEFT : LEFT + cols] = (
            stream[...].astype(jnp.float32).reshape(rows, cols, half)
        )
        each_halo(layer, lambda c: c.wait_recv(), True)
        if layer + 1 < BLOCKS:
            send_weights(layer + 1)
        ends = jnp.dot(spread[...], rim[layer], preferred_element_type=jnp.float32).reshape(
            2, rows + 2 * HALO, LEFT, half
        )
        frame[:, :LEFT] = ends[0]
        frame[:, LEFT + cols :] = ends[1]
        for end, first in ((0, 0), (1, HALO + rows)):
            frame[first : first + HALO, LEFT : LEFT + cols] = (
                band[layer, end].astype(jnp.float32).reshape(HALO, cols, half)
            )

        def shift_row(r, _):
            line = frame[r]
            for e in range(KERNEL):
                first = LEFT - HALO + e
                shifted[e, r] = line[first : first + cols]
            return 0

        lax.fori_loop(0, rows + 2 * HALO, shift_row, 0)

        def conv_row(i, _):
            total = jnp.broadcast_to(conv_bias[layer, 0], (cols, half))
            for a in range(KERNEL):
                for e in range(KERNEL):
                    total = total + shifted[e, i + a] * conv_kernel[layer, a, e]
            at = pl.ds(pl.multiple_of(i * cols, 16), cols)
            conv_all[layer, core, at] = total.astype(jnp.bfloat16)
            return 0

        quarters = 4
        step = rows // quarters
        order = [1, lons - 1] + list(range(2, lons - 1))
        order = order[: lons - 1]

        def conv_copy(q):
            at = pl.ds(q * step * cols, step * cols)
            ref = conv_all.at[layer, core, at]
            return remote(ref, ref, conv_send.at[layer, q], conv_recv.at[layer, q], partner)

        def conv_landed(q):
            at = pl.ds(q * step * cols, step * cols)
            ref = conv_all.at[layer, 1 - core, at]
            return remote(ref, ref, conv_send.at[layer, q], conv_recv.at[layer, q], partner)

        for q in range(quarters):
            lax.fori_loop(q * step, (q + 1) * step, conv_row, 0)
            conv_copy(q).start()
            if q:
                cut = len(order)
                for dz in order[(q - 1) * cut // 3 : q * cut // 3]:
                    pass_on(layer, dz)
        finish_weights(layer)
        for q in range(quarters):
            conv_landed(q).wait_recv()
            conv_copy(q).wait_send()
        each_halo(layer, lambda c: c.wait_send(), False)

        chunk = step * cols

        def part_copy(c):
            at = pl.ds(pl.multiple_of(c * chunk, 16), chunk)
            return remote(
                outgoing.at[layer, at],
                incoming.at[layer, at],
                part_send.at[layer, c],
                part_recv.at[layer, c],
                partner,
            )

        up, down = 2 * layer, 2 * layer + 1
        own = pl.ds(pl.multiple_of(core * half, 128), half)
        other = pl.ds(pl.multiple_of((1 - core) * half, 128), half)
        contract = (((1,), (1,)), ((), ()))

        def ffn(c, _):
            at = pl.ds(pl.multiple_of(c * chunk, 16), chunk)
            conv_f = jnp.concatenate(
                [conv_all[layer, 0, at], conv_all[layer, 1, at]], axis=1
            ).astype(jnp.float32)
            average = jnp.sum(conv_f, axis=1, keepdims=True) / channels
            variance = (
                jnp.sum(conv_f * conv_f, axis=1, keepdims=True) / channels - average * average
            )
            normed = (
                (conv_f - average) * lax.rsqrt(variance + 1e-06) * norm_gain[layer : layer + 1]
                + norm_bias[layer : layer + 1]
            ).astype(jnp.bfloat16)
            pre = jnp.dot(normed, weights[up], preferred_element_type=jnp.float32)
            pre = pre + up_bias[layer : layer + 1, pl.ds(pl.multiple_of(core * hid, 128), hid)]
            hidden = jax.nn.gelu(pre, approximate=True).astype(jnp.bfloat16)
            outgoing[layer, at] = lax.dot_general(
                hidden, weights[down, other], contract, preferred_element_type=jnp.float32
            ).astype(jnp.bfloat16)
            part_copy(c).start()
            mine[at] = lax.dot_general(
                hidden, weights[down, own], contract, preferred_element_type=jnp.float32
            )
            return 0

        lax.fori_loop(0, quarters, ffn, 0)

        def merge(c, _):
            at = pl.ds(pl.multiple_of(c * chunk, 16), chunk)
            part_copy(c).wait_recv()
            update = mine[at] + incoming[layer, at].astype(jnp.float32)
            fresh = stream[at].astype(jnp.float32) + layer_scale[layer : layer + 1, own] * (
                update + down_bias[layer : layer + 1, own]
            )
            if layer + 1 < BLOCKS:
                stream[at] = fresh.astype(jnp.bfloat16)
            else:
                out[at] = fresh.astype(jnp.bfloat16)
            part_copy(c).wait_send()
            return 0

        lax.fori_loop(0, quarters, merge, 0)


def body(
    fields,
    land_sea,
    orography,
    embed_weight,
    class_table,
    conv_kernel,
    conv_bias,
    norm_gain,
    norm_bias,
    up_proj,
    up_bias,
    down_proj,
    down_bias,
    layer_scale,
):
    var_count, lat_cells, lon_cells = fields.shape
    rows = lat_cells // PATCH
    cols = lon_cells // PATCH
    tokens = rows * cols
    channels = norm_gain.shape[1]
    half = embed_weight.shape[3]
    hid = up_proj.shape[2]
    lats, lons, grps = lax.axis_size("lat"), lax.axis_size("lon"), lax.axis_size("grp")
    patches, codes = token_cells(fields, land_sea, orography)
    pack, spread = edge_maps(rows, cols)
    packed = pack.shape[0]
    arrays = 2 * BLOCKS
    helpers = max(lats, grps, 2) - 1
    vmem = pl.BlockSpec(memory_space=pltpu.VMEM)
    dma = pltpu.SemaphoreType.DMA
    result = pl.pallas_call(
        functools.partial(kernel_body, rows, cols),
        out_shape=jax.ShapeDtypeStruct((tokens, half), jnp.bfloat16),
        in_specs=[vmem] * 15,
        out_specs=vmem,
        scratch_shapes=[
            pltpu.VMEM((tokens, half), jnp.bfloat16),
            pltpu.VMEM((BLOCKS, packed, half), jnp.bfloat16),
            pltpu.VMEM((BLOCKS, packed, half), jnp.bfloat16),
            pltpu.VMEM((BLOCKS, 2, HALO * cols, half), jnp.bfloat16),
            pltpu.VMEM((rows + 2 * HALO, cols + 2 * LEFT, half), jnp.float32),
            pltpu.VMEM((KERNEL, rows + 2 * HALO, cols, half), jnp.float32),
            pltpu.VMEM((BLOCKS, 2, tokens, half), jnp.bfloat16),
            pltpu.VMEM((arrays, channels, hid), jnp.bfloat16),
            pltpu.VMEM((tokens, half), jnp.float32),
            pltpu.VMEM((BLOCKS, tokens, half), jnp.bfloat16),
            pltpu.VMEM((BLOCKS, tokens, half), jnp.bfloat16),
            dma((BLOCKS, len(DIRECTIONS))),
            dma((BLOCKS, len(DIRECTIONS))),
            dma((arrays, lons - 1)),
            dma((arrays, lons - 1)),
            dma((arrays, lons - 1, helpers)),
            dma((arrays, lons - 1, helpers)),
            dma((BLOCKS, 4)),
            dma((BLOCKS, 4)),
            dma((BLOCKS, 4)),
            dma((BLOCKS, 4)),
        ],
        compiler_params=pltpu.CompilerParams(
            collective_id=0, has_side_effects=True, vmem_limit_bytes=48 * 1024 * 1024
        ),
    )(
        patches,
        codes,
        embed_weight.transpose(1, 2, 0, 3).reshape(PATCH * PATCH, var_count, half),
        class_table,
        jnp.asarray(pack, jnp.bfloat16),
        jnp.asarray(spread, jnp.bfloat16),
        conv_kernel,
        conv_bias.reshape(BLOCKS, 1, half),
        norm_gain,
        norm_bias,
        up_proj,
        down_proj,
        up_bias,
        down_bias,
        layer_scale,
    )
    return result.reshape(rows, cols, half)


def solution(mesh):
    in_specs = (
        P(None, ("grp", "lat"), "lon"),
        P("lat", "lon"),
        P("lat", "lon"),
        P(None, None, None, "ch"),
        P(None, "ch"),
        P(None, None, None, "ch"),
        P(None, "ch"),
        P(),
        P(),
        P(None, "lon", "ch"),
        P(),
        P(None, "ch", "lon"),
        P(),
        P(),
    )
    out_specs = P(("grp", "lat"), "lon", "ch")
    return jax.shard_map(body, mesh=mesh, in_specs=in_specs, out_specs=out_specs, check_vma=False)
```
